256 devices in a mesh: age: 8 (over z_lo, y), sfh: 32 (over z_hi, x, core).
Axes of the slice: x: 4, y: 4, z: 8 (z_hi: 4, z_lo: 2; z = z_hi * 2 + z_lo), core: 2. Of those that a mesh axis runs over, the one named last changes fastest.
Arguments:
- sfh_weights: bfloat16 [16384, 2048], P('sfh', 'age'), may hold values from 3e-06 to 0.032, as said below
- library: bfloat16 [2048, 5120], P('age', 'sfh'), may hold values from 0.00099 to 100.5, as said below
- kernels: bfloat16 [1280, 160, 64], P(('age', 'sfh')), may hold values from -0.078125 to 0.078125
Outputs:
- photometry: bfloat16 [1280, 16384, 64], P(('age', 'sfh'))
The draws below stay inside these ranges and needn't reach their ends.
Inputs may be any that keep to these rules, and one draw needn't show every extreme that they name: `sfh_weights`: Positive. `library`: Positive.
All inputs are finite; a program needn't handle non-finite values.
Results may differ from the reference program's by a relative error of at most 0.017.
Values may be sent and summed in bfloat16 or wider, within the bound.
A program may use at most 64 MiB of HBM per device.

```python
import math
import jax
import jax.numpy as jnp
from jax import lax

A = 2048
W = 5120
F = 64
ZDEV = 5
S = 16384
Z = 1280
WWIN = 160
N_AGE = 8
N_SFH = 32


log_ten = math.log(10.0)


def age_pattern(key, power):
    base = jax.random.uniform(key, (A,), jnp.float32, -1.0, 1.0)
    return jnp.sign(base) * jnp.abs(base) ** power


def draw_sfh_weights(key, part):
    pattern = age_pattern(key, 1.0)
    key = jax.random.fold_in(key, 11)
    key_slope, key_rough = jax.random.split(key)
    slope = jax.random.uniform(key_slope, (S, 1), jnp.float32, -1.0, 1.0)
    rough = jax.random.uniform(key_rough, (S, A), jnp.float32, -1.0, 1.0)
    exponent = -3.5 + slope * pattern[None, :] + rough
    return jnp.exp(exponent * log_ten).astype(jnp.bfloat16)


def draw_library(key, part):
    pattern = age_pattern(key, 1.0)
    key = jax.random.fold_in(key, 23)
    key_slope, key_rough = jax.random.split(key)
    slope = jax.random.uniform(key_slope, (1, W), jnp.float32, -1.0, 1.0)
    rough = jax.random.uniform(key_rough, (A, W), jnp.float32, -1.0, 1.0)
    exponent = -0.5 + pattern[:, None] * slope + 1.5 * rough
    return jnp.exp(exponent * log_ten).astype(jnp.bfloat16)


def steps_of(key, extent, pieces, least, largest):
    gain = 1.0
    for position, blocks in pieces:
        steps = jax.random.uniform(jax.random.fold_in(jax.random.fold_in(key, 6), position), (blocks,), jnp.float32, least / len(pieces), largest / len(pieces))
        gain = gain * jnp.repeat(jnp.exp(steps), extent[position] // blocks).reshape((-1,) + (1,) * (len(extent) - 1 - position))
    return gain


def normal_values(stream_key, dims, deviation, most, pieces=(), kind=jnp.bfloat16):
    loudness = steps_of(stream_key, dims, pieces, -0.22, 0.18) if pieces else 1.0
    entries = jax.random.normal(stream_key, dims, jnp.float32) * deviation * loudness
    return jnp.minimum(jnp.maximum(entries, -most), most).astype(kind)


def setup_inputs(seed: int = 0) -> dict:
    keys = jax.random.split(jax.random.key(seed), 4)
    sfh_weights = draw_sfh_weights(jax.random.fold_in(keys[3], 71), 0)
    library = draw_library(jax.random.fold_in(keys[3], 71), 0)
    kernels = normal_values(keys[2], (Z, WWIN, F), W ** -0.5, 0.078125, ((0, 256),))
    return dict(sfh_weights=sfh_weights, library=library, kernels=kernels)


def reference(sfh_weights, library, kernels):
    blk = A // N_AGE
    weight_blocks = sfh_weights.reshape(S, N_AGE, blk).transpose(1, 0, 2)
    lib_blocks = library.reshape(N_AGE, blk, W)

    def add_block(total, pair):
        part = jnp.dot(pair[0], pair[1], preferred_element_type=jnp.float32).astype(jnp.bfloat16)
        return total + part.astype(jnp.float32), None

    summed, unused = lax.scan(add_block, jnp.zeros((S, W), jnp.float32), (weight_blocks, lib_blocks))
    composite = summed.astype(jnp.bfloat16)
    grouped = kernels.reshape(N_AGE, N_SFH, ZDEV, WWIN, F)

    def one_window(window):
        cols = lax.dynamic_slice_in_dim(composite, window * WWIN, WWIN, 1).astype(jnp.float32)
        kern = lax.dynamic_index_in_dim(grouped, window, 1, False).astype(jnp.float32)
        return jnp.einsum("sw,azwf->azsf", cols, kern).astype(jnp.bfloat16)

    result = lax.map(one_window, jnp.arange(N_SFH, dtype=jnp.int32))
    result = result.transpose(1, 0, 2, 3, 4)
    return result.reshape(Z, S, F)
```

```python
import functools

import jax
import jax.numpy as jnp
from jax import lax
from jax.experimental import pallas as pl
from jax.experimental.pallas import tpu as pltpu
from jax.sharding import PartitionSpec as P

MESH = pl.DeviceIdType.MESH

NY, NX, NZH = 4, 4, 4
NAGE, NPLANE = 8, 16
ROWS = 128
HALF = 64
KB = 256
WIN = 160

UNITS = {
    (0, 0): 5.0, (0, 3): 10.5, (0, 1): 10.6, (0, 2): 13.5,
    (3, 0): 15.5, (1, 0): 15.6, (3, 3): 20.5, (3, 1): 20.6,
    (3, 2): 23.0, (2, 0): 23.5, (1, 3): 28.0, (1, 1): 28.1,
    (1, 2): 31.0, (2, 3): 36.0, (2, 1): 36.1, (2, 2): 39.0,
}
PACE = 2.4


def schedule():
    events = []
    now = 8.0
    for unit, arrival in sorted(UNITS.items(), key=lambda item: item[1]):
        events.append((arrival, "weights", unit))
        now = max(now, arrival + 1.5)
        events.append((now, "compose", unit))
        events.append((now + 1.8, "pair", unit))
        events.append((now + 4.0, "ring", unit))
        events.append((now + 9.0, "store", unit))
        now += PACE
    return [(kind, unit) for _, kind, unit in sorted(events)]


def gather_kernel(w_ref, l_ref, out_ref, wall, lib, comp, ssem, rsem, a1_send, a1_recv, lib_sem, out_sem):
    age = lax.axis_index("age")
    sfh = lax.axis_index("sfh")
    zl, y = lax.div(age, NY), lax.rem(age, NY)
    core = lax.rem(sfh, 2)
    plane = lax.div(sfh, 2)
    zh, x = lax.div(plane, NX), lax.rem(plane, NX)

    def at(dzl=0, dy=0, dzh=0, dx=0, dc=0):
        a = lax.rem(zl + dzl, 2) * NY + lax.rem(y + dy, NY)
        s = (lax.rem(zh + dzh, NZH) * NX + lax.rem(x + dx, NX)) * 2 + lax.rem(core + dc, 2)
        return (a, s)

    def plane_at(dz, dx):
        return lax.rem(zh + dz, NZH) * NX + lax.rem(x + dx, NX)

    def position(other, dy):
        return lax.rem(zl + other, 2) * NY + lax.rem(y + dy, NY)

    barrier = pltpu.get_barrier_semaphore()
    partners = [at(dzl, dy, 0, 0, dc) for dzl in range(2) for dy in range(NY) for dc in range(2) if (dzl, dy, dc) != (0, 0, 0)]
    partners += [at(dx=1), at(dx=3), at(dzh=1), at(dzh=3)]
    for partner in partners:
        pl.semaphore_signal(barrier, inc=1, device_id=partner, device_id_type=MESH)
    pl.semaphore_wait(barrier, len(partners))

    copies = {}

    def send(name, src, dst, to):
        index = len(copies)
        copy = pltpu.make_async_remote_copy(
            src_ref=src, dst_ref=dst, send_sem=ssem.at[index], recv_sem=rsem.at[index],
            device_id=to, device_id_type=MESH,
        )
        copy.start()
        copies[name] = copy

    def arrived(*name):
        copies[name].wait_recv()

    for q in range(4):
        for h in range(2):
            r = core * 4 + q
            src = w_ref.at[pl.ds(q * ROWS + h * HALF, HALF)]
            dst = wall.at[plane, h, age]
            mine = jnp.logical_and(core == h, r == age)

            @pl.when(mine)
            def _():
                pltpu.make_async_copy(src, dst, a1_recv.at[age]).start()

            @pl.when(jnp.logical_not(mine))
            def _():
                pltpu.make_async_remote_copy(
                    src_ref=src, dst_ref=dst, send_sem=a1_send.at[q * 2 + h], recv_sem=a1_recv.at[age],
                    device_id=(r, plane * 2 + h), device_id_type=MESH,
                ).start()

    own_lib = pltpu.make_async_copy(l_ref, lib.at[age], lib_sem)
    own_lib.start()
    send(("lib", "z"), l_ref, lib.at[age], at(dzl=1))
    send(("lib", "r0"), l_ref, lib.at[age], at(dy=1))
    send(("lib", "l0"), l_ref, lib.at[age], at(dy=3))
    send(("lib", "r1"), l_ref, lib.at[age], at(dzl=1, dy=1))
    send(("lib", "l1"), l_ref, lib.at[age], at(dzl=1, dy=3))

    def weights(unit):
        dz, dx = unit
        p = plane_at(dz, dx)
        part = [wall.at[p, core, pl.ds(0, 4)], wall.at[p, core, pl.ds(4, 4)]]

        def spread(way, half, to):
            send((way, dz, half), part[half], part[half], to)

        if unit == (0, 0):
            for k in range(NAGE):
                pltpu.make_async_copy(w_ref.at[pl.ds(0, HALF)], wall.at[plane, core, k], a1_recv.at[k]).wait()
            spread("x+", 0, at(dx=1))
            spread("x-", 1, at(dx=3))
            spread("z+", 0, at(dzh=1))
            spread("z-", 1, at(dzh=3))
            spread("x+", 1, at(dx=1))
            spread("x-", 0, at(dx=3))
            spread("z+", 1, at(dzh=1))
            spread("z-", 0, at(dzh=3))
        elif dx == 0:
            first = {3: 0, 1: 1, 2: 0}[dz]
            for half in (first, 1 - first):
                if dz == 3:
                    arrived("z+", 0, half)
                    if half == 0:
                        spread("zf+", 0, at(dzh=1))
                elif dz == 1:
                    arrived("z-", 0, half)
                    if half == 1:
                        spread("zf-", 1, at(dzh=3))
                else:
                    arrived(*(("zf+", 3, 0) if half == 0 else ("zf-", 1, 1)))
                spread("x+", half, at(dx=1))
                spread("x-", half, at(dx=3))
        elif dx == 3:
            arrived("x+", dz, 0)
            spread("xf+", 0, at(dx=1))
            arrived("x+", dz, 1)
        elif dx == 1:
            arrived("x-", dz, 1)
            spread("xf-", 1, at(dx=3))
            arrived("x-", dz, 0)
        else:
            arrived("xf+", dz, 0)
            arrived("xf-", dz, 1)
        send(("core", unit), wall.at[p, core], wall.at[p, core], at(dc=1))

    def block(unit, other, dy):
        return comp.at[plane_at(*unit) * NAGE + position(other, dy)]

    def compose(unit):
        arrived("core", unit)
        p = plane_at(*unit)
        total = jnp.zeros((WIN, ROWS), jnp.float32)
        for k in range(NAGE):
            rows = wall[p, :, k].reshape(ROWS, KB)
            total += lax.dot_general(lib[k], rows, (((1,), (1,)), ((), ())), preferred_element_type=jnp.float32)
        comp[p * NAGE + age] = total.astype(jnp.bfloat16)
        mine = block(unit, 0, 0)
        send(("z", unit), mine, mine, at(dzl=1))
        send(("r0", unit), mine, mine, at(dy=1))
        send(("l0", unit), mine, mine, at(dy=3))

    def pair(unit):
        arrived("z", unit)
        theirs = block(unit, 1, 0)
        send(("r1", unit), theirs, theirs, at(dy=1))
        send(("l1", unit), theirs, theirs, at(dy=3))

    def ring(unit):
        arrived("r0", unit)
        left = block(unit, 0, 3)
        send(("f0", unit), left, left, at(dy=1))
        arrived("l1", unit)
        right = block(unit, 1, 1)
        send(("f1", unit), right, right, at(dy=3))

    stores = []

    def store(unit):
        for name in ("l0", "r1", "f0", "f1"):
            arrived(name, unit)
        part = pl.ds(plane_at(*unit) * NAGE, NAGE)
        copy = pltpu.make_async_copy(comp.at[part], out_ref.at[part], out_sem.at[len(stores)])
        copy.start()
        stores.append(copy)

    ready = False
    for kind, unit in schedule():
        if kind == "weights":
            weights(unit)
            if unit == (0, 0):
                arrived("lib", "r0")
                left = lib.at[position(0, 3)]
                send(("lib", "f0"), left, left, at(dy=1))
                arrived("lib", "l1")
                right = lib.at[position(1, 1)]
                send(("lib", "f1"), right, right, at(dy=3))
        elif kind == "compose":
            if not ready:
                own_lib.wait()
                for name in ("z", "l0", "r1", "f0", "f1"):
                    arrived("lib", name)
                ready = True
            compose(unit)
        elif kind == "pair":
            pair(unit)
        elif kind == "ring":
            ring(unit)
        else:
            store(unit)

    for q in range(4):
        for h in range(2):
            mine = jnp.logical_and(core == h, core * 4 + q == age)

            @pl.when(jnp.logical_not(mine))
            def _():
                rows = w_ref.at[pl.ds(q * ROWS + h * HALF, HALF)]
                pltpu.make_async_copy(rows, wall.at[plane, core, 0], a1_send.at[q * 2 + h]).wait()

    for copy in copies.values():
        copy.wait_send()
    for copy in stores:
        copy.wait()


def composites(weights, library_t):
    n_copies = 7 + 30 + 16 + 7 * 16
    return pl.pallas_call(
        gather_kernel,
        out_shape=jax.ShapeDtypeStruct((NPLANE * NAGE, WIN, ROWS), jnp.bfloat16),
        in_specs=[pl.BlockSpec(memory_space=pltpu.VMEM)] * 2,
        out_specs=pl.BlockSpec(memory_space=pl.ANY),
        scratch_shapes=[
            pltpu.VMEM((NPLANE, 2, NAGE, HALF, KB), jnp.bfloat16),
            pltpu.VMEM((NAGE, WIN, KB), jnp.bfloat16),
            pltpu.VMEM((NPLANE * NAGE, WIN, ROWS), jnp.bfloat16),
            pltpu.SemaphoreType.DMA((n_copies,)),
            pltpu.SemaphoreType.DMA((n_copies,)),
            pltpu.SemaphoreType.DMA((8,)),
            pltpu.SemaphoreType.DMA((8,)),
            pltpu.SemaphoreType.DMA,
            pltpu.SemaphoreType.DMA((NPLANE,)),
        ],
        compiler_params=pltpu.CompilerParams(
            collective_id=0, has_side_effects=True, vmem_limit_bytes=40 * 1024 * 1024
        ),
        cost_estimate=pl.CostEstimate(
            flops=2 * 2048 * 2048 * WIN, bytes_accessed=6 * 1024 * 1024, transcendentals=0
        ),
        name="composites",
    )(weights, library_t)


BLOCKS = 16


def photometry_kernel(k_ref, c_ref, o_ref):
    n_z, n_f, n_w = k_ref.shape
    kern = k_ref[...].reshape(n_z * n_f, n_w)
    for b in range(0, BLOCKS, 2):
        cols = jnp.concatenate([c_ref[b], c_ref[b + 1]], axis=1)
        flux = jnp.dot(kern, cols, preferred_element_type=jnp.float32).astype(jnp.bfloat16)
        o_ref[:, :, b * ROWS:(b + 2) * ROWS] = flux.reshape(n_z, n_f, 2 * ROWS)


def photometry(kernels_t, composite):
    n_z, n_f, n_w = kernels_t.shape
    n_blocks = composite.shape[0]
    return pl.pallas_call(
        photometry_kernel,
        grid=(n_blocks // BLOCKS,),
        out_shape=jax.ShapeDtypeStruct((n_z, n_f, n_blocks * ROWS), jnp.bfloat16),
        in_specs=[
            pl.BlockSpec((n_z, n_f, n_w), lambda i: (0, 0, 0)),
            pl.BlockSpec((BLOCKS, n_w, ROWS), lambda i: (i, 0, 0)),
        ],
        out_specs=pl.BlockSpec((n_z, n_f, BLOCKS * ROWS), lambda i: (0, 0, i)),
        compiler_params=pltpu.CompilerParams(vmem_limit_bytes=24 * 1024 * 1024),
        name="photometry",
    )(kernels_t, composite)


def local(sfh_weights, library, kernels):
    composite = composites(sfh_weights, library.T)
    fluxes = photometry(kernels.transpose(0, 2, 1), composite)
    return fluxes.transpose(0, 2, 1)


def solution(mesh):
    placed = (P("sfh", "age"), P("age", "sfh"), P(("age", "sfh"), None, None))
    return jax.shard_map(
        local, mesh=mesh, in_specs=placed, out_specs=P(("age", "sfh"), None, None), check_vma=False
    )
```

```python
import functools

import jax
import jax.numpy as jnp
from jax import lax
from jax.experimental import pallas as pl
from jax.experimental.pallas import tpu as pltpu
from jax.sharding import PartitionSpec as P

MESH = pl.DeviceIdType.MESH

NY, NX, NZH = 4, 4, 4
NAGE, NPLANE = 8, 16
ROWS = 128
HALF = 64
KB = 256
WIN = 160

SENT = {
    "x+": [((0, 0), 0), ((0, 0), 1), ((0, 3), 0), ((3, 0), 0), ((3, 0), 1), ((3, 3), 0),
           ((1, 0), 0), ((1, 0), 1), ((1, 3), 0), ((2, 0), 0), ((2, 0), 1), ((2, 3), 0)],
    "x-": [((0, 0), 1), ((0, 0), 0), ((0, 1), 1), ((1, 0), 1), ((1, 0), 0), ((1, 1), 1),
           ((3, 0), 1), ((3, 0), 0), ((3, 1), 1), ((2, 0), 1), ((2, 0), 0), ((2, 1), 1)],
    "z+": [((0, 0), 0), ((0, 0), 1), ((3, 0), 0)],
    "z-": [((0, 0), 1), ((0, 0), 0), ((1, 0), 1)],
}
STEP = {"x+": (0, 1), "x-": (0, 3), "z+": (1, 0), "z-": (3, 0)}
UNITS = [(0, 0), (0, 3), (0, 1), (0, 2), (3, 0), (1, 0), (3, 3), (1, 1),
         (2, 0), (1, 3), (3, 1), (3, 2), (1, 2), (2, 3), (2, 1), (2, 2)]
CROSS = ((0, 1), (3, 0), (2, 0), (3, 2), (2, 3))
AHEAD = 2
Z_SEND, Z_RECV = (0.0, 0.0, 2.8), (2.8, 3.8, 6.8)
LIBRARY, FIRST, PACE = 1.0, 2.2, 0.8
PAIR_LAG, RING_LAG, STORE_LAG = 2.0, 4.0, 6.0


def schedule():
    events = []
    for n in range(12):
        events.append((max(0, n), "send", ("x+", n)))
        events.append((max(0, n), "send", ("x-", n)))
        events.append((n + AHEAD - 0.1, "take", ("x+", n)))
        events.append((n + AHEAD - 0.1, "take", ("x-", n)))
    for n in range(3):
        for way in ("z+", "z-"):
            events.append((Z_SEND[n] + 0.05, "send", (way, n)))
            events.append((Z_RECV[n], "take", (way, n)))
    events.append((LIBRARY, "library", "pass"))
    events.append((FIRST - 0.01, "library", "wait"))
    for k, unit in enumerate(UNITS):
        now = FIRST + PACE * k
        events.append((now, "compose", unit))
        events.append((now + PAIR_LAG, "turn" if unit in CROSS else "pair", unit))
        events.append((now + RING_LAG, "cross" if unit in CROSS else "ring", unit))
        events.append((now + STORE_LAG, "store", unit))
    order = sorted(range(len(events)), key=lambda e: events[e][0])
    return [events[e][1:] for e in order]


def gather_kernel(w_ref, l_ref, out_ref, wall, lib, comp, ssem, rsem, a1_send, a1_recv, lib_sem, out_sem):
    age = lax.axis_index("age")
    sfh = lax.axis_index("sfh")
    zl, y = lax.div(age, NY), lax.rem(age, NY)
    core = lax.rem(sfh, 2)
    plane = lax.div(sfh, 2)
    zh, x = lax.div(plane, NX), lax.rem(plane, NX)

    def at(dzl=0, dy=0, dzh=0, dx=0, dc=0):
        a = lax.rem(zl + dzl, 2) * NY + lax.rem(y + dy, NY)
        s = (lax.rem(zh + dzh, NZH) * NX + lax.rem(x + dx, NX)) * 2 + lax.rem(core + dc, 2)
        return (a, s)

    def plane_at(dz, dx):
        return lax.rem(zh + dz, NZH) * NX + lax.rem(x + dx, NX)

    def position(other, dy):
        return lax.rem(zl + other, 2) * NY + lax.rem(y + dy, NY)

    barrier = pltpu.get_barrier_semaphore()
    partners = [at(dzl, dy, 0, 0, dc) for dzl in range(2) for dy in range(NY) for dc in range(2) if (dzl, dy, dc) != (0, 0, 0)]
    partners += [at(dx=1), at(dx=3), at(dzh=1), at(dzh=3)]
    for partner in partners:
        pl.semaphore_signal(barrier, inc=1, device_id=partner, device_id_type=MESH)
    pl.semaphore_wait(barrier, len(partners))

    copies = {}

    def send(name, src, dst, to):
        index = len(copies)
        copy = pltpu.make_async_remote_copy(
            src_ref=src, dst_ref=dst, send_sem=ssem.at[index], recv_sem=rsem.at[index],
            device_id=to, device_id_type=MESH,
        )
        copy.start()
        copies[name] = copy

    def arrived(*name):
        copies[name].wait_recv()

    for q in range(4):
        for h in range(2):
            r = core * 4 + q
            src = w_ref.at[pl.ds(q * ROWS + h * HALF, HALF)]
            dst = wall.at[plane, h, age]
            mine = jnp.logical_and(core == h, r == age)

            @pl.when(mine)
            def _():
                pltpu.make_async_copy(src, dst, a1_recv.at[age]).start()

            @pl.when(jnp.logical_not(mine))
            def _():
                pltpu.make_async_remote_copy(
                    src_ref=src, dst_ref=dst, send_sem=a1_send.at[q * 2 + h], recv_sem=a1_recv.at[age],
                    device_id=(r, plane * 2 + h), device_id_type=MESH,
                ).start()

    own_lib = pltpu.make_async_copy(l_ref, lib.at[age], lib_sem)
    own_lib.start()
    send(("lib", "z"), l_ref, lib.at[age], at(dzl=1))
    send(("lib", "r0"), l_ref, lib.at[age], at(dy=1))
    send(("lib", "l0"), l_ref, lib.at[age], at(dy=3))
    send(("lib", "r1"), l_ref, lib.at[age], at(dzl=1, dy=1))
    send(("lib", "l1"), l_ref, lib.at[age], at(dzl=1, dy=3))

    def library(what):
        if what == "pass":
            arrived("lib", "r0")
            left = lib.at[position(0, 3)]
            send(("lib", "f0"), left, left, at(dy=1))
            arrived("lib", "l1")
            right = lib.at[position(1, 1)]
            send(("lib", "f1"), right, right, at(dy=3))
        else:
            own_lib.wait()
            for name in ("z", "l0", "r1", "f0", "f1"):
                arrived("lib", name)

    def pass_on(unit, half):
        part = wall.at[plane_at(*unit), core, pl.ds(half * 4, 4)]
        send(("core", unit, half), part, part, at(dc=1))

    def send_weights(way, n):
        unit, half = SENT[way][n]
        part = wall.at[plane_at(*unit), core, pl.ds(half * 4, 4)]
        dz, dx = STEP[way]
        send((way, n), part, part, at(dzh=dz, dx=dx))

    def take_weights(way, n):
        (dz, dx), half = SENT[way][n]
        arrived(way, n)
        pass_on(((dz - STEP[way][0]) % 4, (dx - STEP[way][1]) % 4), half)

    def block(unit, other, dy):
        return comp.at[plane_at(*unit) * NAGE + position(other, dy)]

    def compose(unit):
        arrived("core", unit, 0)
        arrived("core", unit, 1)
        p = plane_at(*unit)
        total = jnp.zeros((WIN, ROWS), jnp.float32)
        for k in range(NAGE):
            rows = wall[p, :, k].reshape(ROWS, KB)
            total += lax.dot_general(lib[k], rows, (((1,), (1,)), ((), ())), preferred_element_type=jnp.float32)
        comp[p * NAGE + age] = total.astype(jnp.bfloat16)
        mine = block(unit, 0, 0)
        send(("z", unit), mine, mine, at(dzl=1))
        send(("r0", unit), mine, mine, at(dy=1))
        send(("l0", unit), mine, mine, at(dy=3))

    def pair(unit):
        arrived("z", unit)
        theirs = block(unit, 1, 0)
        send(("r1", unit), theirs, theirs, at(dy=1))
        send(("l1", unit), theirs, theirs, at(dy=3))

    def ring(unit):
        arrived("r0", unit)
        left = block(unit, 0, 3)
        send(("f0", unit), left, left, at(dy=1))
        arrived("l1", unit)
        right = block(unit, 1, 1)
        send(("f1", unit), right, right, at(dy=3))

    def turn(unit):
        right_way = CROSS.index(unit) % 2 == 0
        arrived("r0", unit)
        left = block(unit, 0, 3)
        if right_way:
            send(("f0", unit), left, left, at(dy=1))
        send(("zl", unit), left, left, at(dzl=1))
        arrived("l0", unit)
        right = block(unit, 0, 1)
        if not right_way:
            send(("f0", unit), right, right, at(dy=3))
        send(("zr", unit), right, right, at(dzl=1))

    def cross(unit):
        arrived("f0", unit)
        far = block(unit, 0, 2)
        send(("zf", unit), far, far, at(dzl=1))

    stores = []

    def store(unit):
        for name in ("z", "zl", "zr", "zf") if unit in CROSS else ("l0", "r1", "f0", "f1"):
            arrived(name, unit)
        part = pl.ds(plane_at(*unit) * NAGE, NAGE)
        copy = pltpu.make_async_copy(comp.at[part], out_ref.at[part], out_sem.at[len(stores)])
        copy.start()
        stores.append(copy)

    for k in range(NAGE):
        pltpu.make_async_copy(w_ref.at[pl.ds(0, HALF)], wall.at[plane, core, k], a1_recv.at[k]).wait()
    pass_on((0, 0), 0)
    pass_on((0, 0), 1)

    for kind, what in schedule():
        if kind == "send":
            send_weights(*what)
        elif kind == "take":
            take_weights(*what)
        elif kind == "library":
            library(what)
        elif kind == "compose":
            compose(what)
        elif kind == "pair":
            pair(what)
        elif kind == "ring":
            ring(what)
        elif kind == "turn":
            turn(what)
        elif kind == "cross":
            cross(what)
        else:
            store(what)

    for q in range(4):
        for h in range(2):
            mine = jnp.logical_and(core == h, core * 4 + q == age)

            @pl.when(jnp.logical_not(mine))
            def _():
                rows = w_ref.at[pl.ds(q * ROWS + h * HALF, HALF)]
                pltpu.make_async_copy(rows, wall.at[plane, core, 0], a1_send.at[q * 2 + h]).wait()

    for copy in copies.values():
        copy.wait_send()
    for copy in stores:
        copy.wait()


def composites(weights, library_t):
    n_copies = 7 + 30 + 32 + 7 * 16
    return pl.pallas_call(
        gather_kernel,
        out_shape=jax.ShapeDtypeStruct((NPLANE * NAGE, WIN, ROWS), jnp.bfloat16),
        in_specs=[pl.BlockSpec(memory_space=pltpu.HBM)] * 2,
        out_specs=pl.BlockSpec(memory_space=pl.ANY),
        scratch_shapes=[
            pltpu.VMEM((NPLANE, 2, NAGE, HALF, KB), jnp.bfloat16),
            pltpu.VMEM((NAGE, WIN, KB), jnp.bfloat16),
            pltpu.VMEM((NPLANE * NAGE, WIN, ROWS), jnp.bfloat16),
            pltpu.SemaphoreType.DMA((n_copies,)),
            pltpu.SemaphoreType.DMA((n_copies,)),
            pltpu.SemaphoreType.DMA((8,)),
            pltpu.SemaphoreType.DMA((8,)),
            pltpu.SemaphoreType.DMA,
            pltpu.SemaphoreType.DMA((NPLANE,)),
        ],
        compiler_params=pltpu.CompilerParams(
            collective_id=0, has_side_effects=True, vmem_limit_bytes=24 * 1024 * 1024
        ),
        cost_estimate=pl.CostEstimate(
            flops=2 * 2048 * 2048 * WIN, bytes_accessed=6 * 1024 * 1024, transcendentals=0
        ),
        name="composites",
    )(weights, library_t)


BLOCKS = 32


def photometry_kernel(k_ref, c_ref, o_ref):
    n_z, n_f, n_w = k_ref.shape
    kern = k_ref[...].reshape(n_z * n_f, n_w)
    first = pl.program_id(0) * BLOCKS
    for b in range(0, BLOCKS, 2):
        cols = jnp.concatenate([c_ref[first + b], c_ref[first + b + 1]], axis=1)
        flux = jnp.dot(kern, cols, preferred_element_type=jnp.float32).astype(jnp.bfloat16)
        o_ref[:, :, b * ROWS:(b + 2) * ROWS] = flux.reshape(n_z, n_f, 2 * ROWS)


def photometry(kernels_t, composite):
    n_z, n_f, n_w = kernels_t.shape
    n_blocks = composite.shape[0]
    return pl.pallas_call(
        photometry_kernel,
        grid=(n_blocks // BLOCKS,),
        out_shape=jax.ShapeDtypeStruct((n_z, n_f, n_blocks * ROWS), jnp.bfloat16),
        in_specs=[
            pl.BlockSpec((n_z, n_f, n_w), lambda i: (0, 0, 0)),
            pl.BlockSpec(memory_space=pltpu.VMEM),
        ],
        out_specs=pl.BlockSpec((n_z, n_f, BLOCKS * ROWS), lambda i: (0, 0, i)),
        compiler_params=pltpu.CompilerParams(vmem_limit_bytes=24 * 1024 * 1024),
        name="photometry",
    )(kernels_t, composite)


def local(sfh_weights, library, kernels):
    composite = composites(sfh_weights, library.T)
    fluxes = photometry(kernels.transpose(0, 2, 1), composite)
    return fluxes.transpose(0, 2, 1)


def solution(mesh):
    placed = (P("sfh", "age"), P("age", "sfh"), P(("age", "sfh"), None, None))
    return jax.shard_map(
        local, mesh=mesh, in_specs=placed, out_specs=P(("age", "sfh"), None, None), check_vma=False
    )
```

```python
import functools

import jax
import jax.numpy as jnp
from jax import lax
from jax.experimental import pallas as pl
from jax.experimental.pallas import tpu as pltpu
from jax.sharding import PartitionSpec as P

MESH = pl.DeviceIdType.MESH

NY, NX, NZH = 4, 4, 4
NAGE, NPLANE = 8, 16
ROWS = 128
HALF = 64
KB = 256
WIN = 160

SENT = {
    "x+": [((0, 0), 0), ((0, 0), 1), ((0, 3), 0), ((3, 0), 0), ((1, 0), 1), ((3, 0), 1),
           ((1, 0), 0), ((3, 3), 0), ((1, 3), 0), ((2, 0), 0), ((2, 0), 1), ((2, 3), 0)],
    "x-": [((0, 0), 1), ((0, 0), 0), ((0, 1), 1), ((1, 0), 1), ((3, 0), 0), ((1, 0), 0),
           ((3, 0), 1), ((1, 1), 1), ((3, 1), 1), ((2, 0), 1), ((2, 0), 0), ((2, 1), 1)],
    "z+": [((0, 0), 0), ((0, 0), 1), ((3, 0), 0)],
    "z-": [((0, 0), 1), ((0, 0), 0), ((1, 0), 1)],
}
STEP = {"x+": (0, 1), "x-": (0, 3), "z+": (1, 0), "z-": (3, 0)}
UNITS = [(0, 0), (0, 3), (0, 1), (0, 2), (3, 0), (1, 0), (3, 3), (1, 1),
         (1, 3), (3, 1), (2, 0), (3, 2), (1, 2), (2, 3), (2, 1), (2, 2)]
CROSS = ((0, 1), (3, 0), (1, 1), (3, 1), (3, 2), (2, 3))
AHEAD = 2
FAR_FIRST = (2, 1, 3, 0)
Z_SEND, Z_RECV = (-0.05, 1.0, 2.9), (2.85, 4.85, 8.8)
LIBRARY, TURN, FIRST, PACE = 0.05, 0.8, 2.2, 0.8
PAIR_LAG, RING_LAG, STORE_LAG = 2.0, 4.0, 6.0


def schedule():
    events = []
    for n in range(12):
        events.append((max(0, n), "send", ("x+", n)))
        events.append((max(0, n), "send", ("x-", n)))
        events.append((n + AHEAD - 0.1, "take", ("x+", n)))
        events.append((n + AHEAD - 0.1, "take", ("x-", n)))
    for n in range(3):
        for way in ("z+", "z-"):
            events.append((Z_SEND[n], "send", (way, n)))
            events.append((Z_RECV[n], "take", (way, n)))
    events += [(0.01, "pass", ((0, 0), half)) for half in range(2)]
    events.append((LIBRARY, "library", "pass"))
    events.append((TURN, "library", "turn"))
    events.append((FIRST - 0.01, "library", "wait"))
    for k, unit in enumerate(UNITS):
        now = FIRST + PACE * k
        events.append((now, "compose", unit))
        events.append((now + PAIR_LAG, "turn" if unit in CROSS else "pair", unit))
        events.append((now + RING_LAG, "cross" if unit in CROSS else "ring", unit))
        events.append((now + STORE_LAG, "store", unit))
    order = sorted(range(len(events)), key=lambda e: events[e][0])
    return [events[e][1:] for e in order]


def gather_kernel(w_ref, l_ref, out_ref, wall, lib, comp, ssem, rsem, a1_send, a1_recv, lib_sem, out_sem):
    age = lax.axis_index("age")
    sfh = lax.axis_index("sfh")
    zl, y = lax.div(age, NY), lax.rem(age, NY)
    core = lax.rem(sfh, 2)
    plane = lax.div(sfh, 2)
    zh, x = lax.div(plane, NX), lax.rem(plane, NX)

    def at(dzl=0, dy=0, dzh=0, dx=0, dc=0):
        a = lax.rem(zl + dzl, 2) * NY + lax.rem(y + dy, NY)
        s = (lax.rem(zh + dzh, NZH) * NX + lax.rem(x + dx, NX)) * 2 + lax.rem(core + dc, 2)
        return (a, s)

    def plane_at(dz, dx):
        return lax.rem(zh + dz, NZH) * NX + lax.rem(x + dx, NX)

    def position(other, dy):
        return lax.rem(zl + other, 2) * NY + lax.rem(y + dy, NY)

    barrier = pltpu.get_barrier_semaphore()
    partners = [at(dzl, dy, 0, 0, dc) for dzl in range(2) for dy in range(NY) for dc in range(2) if (dzl, dy, dc) != (0, 0, 0)]
    partners += [at(dx=1), at(dx=3), at(dzh=1), at(dzh=3)]
    for partner in partners:
        pl.semaphore_signal(barrier, inc=1, device_id=partner, device_id_type=MESH)
    pl.semaphore_wait(barrier, len(partners))

    copies = {}

    def send(name, src, dst, to):
        index = len(copies)
        copy = pltpu.make_async_remote_copy(
            src_ref=src, dst_ref=dst, send_sem=ssem.at[index], recv_sem=rsem.at[index],
            device_id=to, device_id_type=MESH,
        )
        copy.start()
        copies[name] = copy

    def arrived(*name):
        copies[name].wait_recv()

    for n, dy in enumerate(FAR_FIRST):
        q = lax.rem(y + dy, NY)
        r = core * 4 + q
        for h in range(2):
            src = w_ref.at[pl.ds(pl.multiple_of(q * ROWS + h * HALF, HALF), HALF)]
            dst = wall.at[plane, h, age]
            mine = jnp.logical_and(core == h, r == age)

            @pl.when(mine)
            def _():
                pltpu.make_async_copy(src, dst, a1_recv.at[age]).start()

            @pl.when(jnp.logical_not(mine))
            def _():
                pltpu.make_async_remote_copy(
                    src_ref=src, dst_ref=dst, send_sem=a1_send.at[n * 2 + h], recv_sem=a1_recv.at[age],
                    device_id=(r, plane * 2 + h), device_id_type=MESH,
                ).start()

    own_lib = pltpu.make_async_copy(l_ref, lib.at[age], lib_sem)
    own_lib.start()
    send(("lib", "z"), l_ref, lib.at[age], at(dzl=1))
    send(("lib", "r0"), l_ref, lib.at[age], at(dy=1))
    send(("lib", "l0"), l_ref, lib.at[age], at(dy=3))

    def library(what):
        if what == "pass":
            arrived("lib", "z")
            theirs = lib.at[position(1, 0)]
            send(("lib", "r1"), theirs, theirs, at(dy=1))
            send(("lib", "l1"), theirs, theirs, at(dy=3))
            arrived("lib", "r0")
            left = lib.at[position(0, 3)]
            send(("lib", "f0"), left, left, at(dy=1))
        elif what == "turn":
            arrived("lib", "l1")
            right = lib.at[position(1, 1)]
            send(("lib", "f1"), right, right, at(dy=3))
        else:
            own_lib.wait()
            for name in ("l0", "r1", "f0", "f1"):
                arrived("lib", name)

    def pass_on(unit, half):
        part = wall.at[plane_at(*unit), core, pl.ds(half * 4, 4)]
        send(("core", unit, half), part, part, at(dc=1))

    def send_weights(way, n):
        unit, half = SENT[way][n]
        part = wall.at[plane_at(*unit), core, pl.ds(half * 4, 4)]
        dz, dx = STEP[way]
        send((way, n), part, part, at(dzh=dz, dx=dx))

    def take_weights(way, n):
        (dz, dx), half = SENT[way][n]
        arrived(way, n)
        pass_on(((dz - STEP[way][0]) % 4, (dx - STEP[way][1]) % 4), half)

    def block(unit, other, dy):
        return comp.at[plane_at(*unit) * NAGE + position(other, dy)]

    def compose(unit):
        arrived("core", unit, 0)
        arrived("core", unit, 1)
        p = plane_at(*unit)
        total = jnp.zeros((WIN, ROWS), jnp.float32)
        for k in range(NAGE):
            rows = wall[p, :, k].reshape(ROWS, KB)
            total += lax.dot_general(lib[k], rows, (((1,), (1,)), ((), ())), preferred_element_type=jnp.float32)
        comp[p * NAGE + age] = total.astype(jnp.bfloat16)
        mine = block(unit, 0, 0)
        send(("z", unit), mine, mine, at(dzl=1))
        send(("r0", unit), mine, mine, at(dy=1))
        send(("l0", unit), mine, mine, at(dy=3))

    def pair(unit):
        arrived("z", unit)
        theirs = block(unit, 1, 0)
        send(("r1", unit), theirs, theirs, at(dy=1))
        send(("l1", unit), theirs, theirs, at(dy=3))

    def ring(unit):
        arrived("r0", unit)
        left = block(unit, 0, 3)
        send(("f0", unit), left, left, at(dy=1))
        arrived("l1", unit)
        right = block(unit, 1, 1)
        send(("f1", unit), right, right, at(dy=3))

    def turn(unit):
        right_way = CROSS.index(unit) % 2 == 0
        arrived("r0", unit)
        left = block(unit, 0, 3)
        if right_way:
            send(("f0", unit), left, left, at(dy=1))
        send(("zl", unit), left, left, at(dzl=1))
        arrived("l0", unit)
        right = block(unit, 0, 1)
        if not right_way:
            send(("f0", unit), right, right, at(dy=3))
        send(("zr", unit), right, right, at(dzl=1))

    def cross(unit):
        arrived("f0", unit)
        far = block(unit, 0, 2)
        send(("zf", unit), far, far, at(dzl=1))

    stores = []

    def store(unit):
        for name in ("z", "zl", "zr", "zf") if unit in CROSS else ("l0", "r1", "f0", "f1"):
            arrived(name, unit)
        part = pl.ds(plane_at(*unit) * NAGE, NAGE)
        copy = pltpu.make_async_copy(comp.at[part], out_ref.at[part], out_sem.at[len(stores)])
        copy.start()
        stores.append(copy)

    for k in range(NAGE):
        pltpu.make_async_copy(w_ref.at[pl.ds(0, HALF)], wall.at[plane, core, k], a1_recv.at[k]).wait()
    for kind, what in schedule():
        if kind == "send":
            send_weights(*what)
        elif kind == "take":
            take_weights(*what)
        elif kind == "pass":
            pass_on(*what)
        elif kind == "library":
            library(what)
        elif kind == "compose":
            compose(what)
        elif kind == "pair":
            pair(what)
        elif kind == "ring":
            ring(what)
        elif kind == "turn":
            turn(what)
        elif kind == "cross":
            cross(what)
        else:
            store(what)

    for n, dy in enumerate(FAR_FIRST):
        for h in range(2):
            mine = jnp.logical_and(core == h, core * 4 + lax.rem(y + dy, NY) == age)

            @pl.when(jnp.logical_not(mine))
            def _():
                rows = w_ref.at[pl.ds(0, HALF)]
                pltpu.make_async_copy(rows, wall.at[plane, core, 0], a1_send.at[n * 2 + h]).wait()

    for copy in copies.values():
        copy.wait_send()
    for copy in stores:
        copy.wait()


def composites(weights, library_t):
    n_copies = 7 + 30 + 32 + 7 * 16
    return pl.pallas_call(
        gather_kernel,
        out_shape=jax.ShapeDtypeStruct((NPLANE * NAGE, WIN, ROWS), jnp.bfloat16),
        in_specs=[pl.BlockSpec(memory_space=pltpu.HBM)] * 2,
        out_specs=pl.BlockSpec(memory_space=pl.ANY),
        scratch_shapes=[
            pltpu.VMEM((NPLANE, 2, NAGE, HALF, KB), jnp.bfloat16),
            pltpu.VMEM((NAGE, WIN, KB), jnp.bfloat16),
            pltpu.VMEM((NPLANE * NAGE, WIN, ROWS), jnp.bfloat16),
            pltpu.SemaphoreType.DMA((n_copies,)),
            pltpu.SemaphoreType.DMA((n_copies,)),
            pltpu.SemaphoreType.DMA((8,)),
            pltpu.SemaphoreType.DMA((8,)),
            pltpu.SemaphoreType.DMA,
            pltpu.SemaphoreType.DMA((NPLANE,)),
        ],
        compiler_params=pltpu.CompilerParams(
            collective_id=0, has_side_effects=True, vmem_limit_bytes=24 * 1024 * 1024
        ),
        cost_estimate=pl.CostEstimate(
            flops=2 * 2048 * 2048 * WIN, bytes_accessed=6 * 1024 * 1024, transcendentals=0
        ),
        name="composites",
    )(weights, library_t)


BLOCKS = 32


def photometry_kernel(k_ref, c_ref, o_ref):
    n_z, n_f, n_w = k_ref.shape
    kern = k_ref[...].reshape(n_z * n_f, n_w)
    first = pl.program_id(0) * BLOCKS
    for b in range(0, BLOCKS, 2):
        cols = jnp.concatenate([c_ref[first + b], c_ref[first + b + 1]], axis=1)
        flux = jnp.dot(kern, cols, preferred_element_type=jnp.float32).astype(jnp.bfloat16)
        o_ref[:, :, b * ROWS:(b + 2) * ROWS] = flux.reshape(n_z, n_f, 2 * ROWS)


def photometry(kernels_t, composite):
    n_z, n_f, n_w = kernels_t.shape
    n_blocks = composite.shape[0]
    return pl.pallas_call(
        photometry_kernel,
        grid=(n_blocks // BLOCKS,),
        out_shape=jax.ShapeDtypeStruct((n_z, n_f, n_blocks * ROWS), jnp.bfloat16),
        in_specs=[
            pl.BlockSpec((n_z, n_f, n_w), lambda i: (0, 0, 0)),
            pl.BlockSpec(memory_space=pltpu.VMEM),
        ],
        out_specs=pl.BlockSpec((n_z, n_f, BLOCKS * ROWS), lambda i: (0, 0, i)),
        compiler_params=pltpu.CompilerParams(vmem_limit_bytes=24 * 1024 * 1024),
        name="photometry",
    )(kernels_t, composite)


def local(sfh_weights, library, kernels):
    composite = composites(sfh_weights, library.T)
    fluxes = photometry(kernels.transpose(0, 2, 1), composite)
    return fluxes.transpose(0, 2, 1)


def solution(mesh):
    placed = (P("sfh", "age"), P("age", "sfh"), P(("age", "sfh"), None, None))
    return jax.shard_map(
        local, mesh=mesh, in_specs=placed, out_specs=P(("age", "sfh"), None, None), check_vma=False
    )
```

```python
import functools

import jax
import jax.numpy as jnp
from jax import lax
from jax.experimental import pallas as pl
from jax.experimental.pallas import tpu as pltpu
from jax.sharding import PartitionSpec as P

MESH = pl.DeviceIdType.MESH

NY, NX, NZH = 4, 4, 4
NAGE, NPLANE = 8, 16
ROWS = 128
HALF = 64
KB = 256
WIN = 160

SENT = {
    "x+": [((0, 0), 0), ((0, 0), 1), ((0, 3), 0), ((3, 0), 0), ((1, 0), 1), ((3, 0), 1),
           ((1, 0), 0), ((3, 3), 0), ((1, 3), 0), ((2, 0), 0), ((2, 0), 1), ((2, 3), 0)],
    "x-": [((0, 0), 1), ((0, 0), 0), ((0, 1), 1), ((1, 0), 1), ((3, 0), 0), ((1, 0), 0),
           ((3, 0), 1), ((1, 1), 1), ((3, 1), 1), ((2, 0), 1), ((2, 0), 0), ((2, 1), 1)],
    "z+": [((0, 0), 0), ((0, 0), 1), ((3, 0), 0)],
    "z-": [((0, 0), 1), ((0, 0), 0), ((1, 0), 1)],
}
STEP = {"x+": (0, 1), "x-": (0, 3), "z+": (1, 0), "z-": (3, 0)}
UNITS = [(0, 0), (0, 3), (0, 1), (0, 2), (3, 0), (1, 0), (3, 3), (1, 1),
         (1, 3), (3, 1), (2, 0), (3, 2), (1, 2), (2, 3), (2, 1), (2, 2)]
CROSS = ((0, 1), (3, 0), (1, 1), (3, 1), (3, 2), (2, 3))
AHEAD = 2
FAR_FIRST = (2, 1, 3, 0)
Z_SEND, Z_RECV = (-0.05, 1.0, 2.9), (2.85, 4.85, 8.8)
LIBRARY, TURN, FIRST, PACE = 0.05, 0.8, 2.2, 0.65
PAIR_LAG, RING_LAG, STORE_LAG = 2.0, 4.0, 6.0
SETTLE = 0.5


def schedule():
    events = []
    for n in range(12):
        events.append((n or -0.24, "send", ("x+", n)))
        events.append((n or -0.04, "send", ("x-", n)))
        events.append((n + AHEAD - 0.1, "take", ("x+", n)))
        events.append((n + AHEAD - 0.1, "take", ("x-", n)))
    for n in range(3):
        for way in ("z+", "z-"):
            early = 0.2 if (way, n) == ("z+", 0) else 0.0
            events.append((Z_SEND[n] - early, "send", (way, n)))
            events.append((Z_RECV[n], "take", (way, n)))
    events += [(-0.3, "own", 0), (-0.2, "own", 1)]
    events += [(0.01, "pass", ((0, 0), half)) for half in range(2)]
    events.append((LIBRARY, "library", "pass"))
    events.append((TURN, "library", "turn"))
    events.append((FIRST - 0.01, "library", "wait"))
    ready = {}
    for moment, kind, what in events:
        if kind == "take":
            (dz, dx), _ = SENT[what[0]][what[1]]
            unit = ((dz - STEP[what[0]][0]) % 4, (dx - STEP[what[0]][1]) % 4)
            ready[unit] = max(ready.get(unit, 0.0), moment + SETTLE)
    now = FIRST - PACE
    for unit in UNITS:
        now = max(now + PACE, ready.get(unit, 0.0))
        events.append((now, "compose", unit))
        events.append((now + PAIR_LAG, "turn" if unit in CROSS else "pair", unit))
        events.append((now + RING_LAG, "cross" if unit in CROSS else "ring", unit))
        events.append((now + STORE_LAG, "store", unit))
    order = sorted(range(len(events)), key=lambda e: events[e][0])
    return [events[e][1:] for e in order]


def gather_kernel(
    w_ref, l_ref, k_ref, out_ref, k_out, wall, lib, comp, ssem, rsem, a1_send, a1_recv, lib_sem, k_sem, out_sem
):
    age = lax.axis_index("age")
    sfh = lax.axis_index("sfh")
    zl, y = lax.div(age, NY), lax.rem(age, NY)
    core = lax.rem(sfh, 2)
    plane = lax.div(sfh, 2)
    zh, x = lax.div(plane, NX), lax.rem(plane, NX)

    def at(dzl=0, dy=0, dzh=0, dx=0, dc=0):
        a = lax.rem(zl + dzl, 2) * NY + lax.rem(y + dy, NY)
        s = (lax.rem(zh + dzh, NZH) * NX + lax.rem(x + dx, NX)) * 2 + lax.rem(core + dc, 2)
        return (a, s)

    def plane_at(dz, dx):
        return lax.rem(zh + dz, NZH) * NX + lax.rem(x + dx, NX)

    def position(other, dy):
        return lax.rem(zl + other, 2) * NY + lax.rem(y + dy, NY)

    barrier = pltpu.get_barrier_semaphore()
    partners = [at(dzl, dy, 0, 0, dc) for dzl in range(2) for dy in range(NY) for dc in range(2) if (dzl, dy, dc) != (0, 0, 0)]
    partners += [at(dx=1), at(dx=3), at(dzh=1), at(dzh=3)]
    for partner in partners:
        pl.semaphore_signal(barrier, inc=1, device_id=partner, device_id_type=MESH)
    pl.semaphore_wait(barrier, len(partners))

    copies = {}

    def send(name, src, dst, to):
        index = len(copies)
        copy = pltpu.make_async_remote_copy(
            src_ref=src, dst_ref=dst, send_sem=ssem.at[index], recv_sem=rsem.at[index],
            device_id=to, device_id_type=MESH,
        )
        copy.start()
        copies[name] = copy

    def arrived(*name):
        copies[name].wait_recv()

    for n, dy in enumerate(FAR_FIRST):
        q = lax.rem(y + dy, NY)
        r = core * 4 + q
        for h in range(2):
            src = w_ref.at[pl.ds(pl.multiple_of(q * ROWS + h * HALF, HALF), HALF)]
            dst = wall.at[plane, h, age]
            mine = jnp.logical_and(core == h, r == age)

            @pl.when(mine)
            def _():
                pltpu.make_async_copy(src, dst, a1_recv.at[age]).start()

            @pl.when(jnp.logical_not(mine))
            def _():
                pltpu.make_async_remote_copy(
                    src_ref=src, dst_ref=dst, send_sem=a1_send.at[n * 2 + h], recv_sem=a1_recv.at[age],
                    device_id=(r, plane * 2 + h), device_id_type=MESH,
                ).start()

    own_lib = pltpu.make_async_copy(l_ref, lib.at[age], lib_sem)
    own_lib.start()
    bring = pltpu.make_async_copy(k_ref, k_out, k_sem)
    bring.start()
    send(("lib", "z"), l_ref, lib.at[age], at(dzl=1))
    send(("lib", "r0"), l_ref, lib.at[age], at(dy=1))
    send(("lib", "l0"), l_ref, lib.at[age], at(dy=3))

    def library(what):
        if what == "pass":
            arrived("lib", "z")
            theirs = lib.at[position(1, 0)]
            send(("lib", "r1"), theirs, theirs, at(dy=1))
            send(("lib", "l1"), theirs, theirs, at(dy=3))
            arrived("lib", "r0")
            left = lib.at[position(0, 3)]
            send(("lib", "f0"), left, left, at(dy=1))
        elif what == "turn":
            arrived("lib", "l1")
            right = lib.at[position(1, 1)]
            send(("lib", "f1"), right, right, at(dy=3))
        else:
            own_lib.wait()
            for name in ("l0", "r1", "f0", "f1"):
                arrived("lib", name)

    def pass_on(unit, half):
        part = wall.at[plane_at(*unit), core, pl.ds(half * 4, 4)]
        send(("core", unit, half), part, part, at(dc=1))

    def send_weights(way, n):
        unit, half = SENT[way][n]
        part = wall.at[plane_at(*unit), core, pl.ds(half * 4, 4)]
        dz, dx = STEP[way]
        send((way, n), part, part, at(dzh=dz, dx=dx))

    def take_weights(way, n):
        (dz, dx), half = SENT[way][n]
        arrived(way, n)
        pass_on(((dz - STEP[way][0]) % 4, (dx - STEP[way][1]) % 4), half)

    def block(unit, other, dy):
        return comp.at[plane_at(*unit) * NAGE + position(other, dy)]

    def compose(unit):
        arrived("core", unit, 0)
        arrived("core", unit, 1)
        p = plane_at(*unit)
        total = jnp.zeros((WIN, ROWS), jnp.float32)
        for k in range(NAGE):
            rows = wall[p, :, k].reshape(ROWS, KB)
            total += lax.dot_general(lib[k], rows, (((1,), (1,)), ((), ())), preferred_element_type=jnp.float32)
        comp[p * NAGE + age] = total.astype(jnp.bfloat16)
        mine = block(unit, 0, 0)
        send(("z", unit), mine, mine, at(dzl=1))
        send(("r0", unit), mine, mine, at(dy=1))
        send(("l0", unit), mine, mine, at(dy=3))

    def pair(unit):
        arrived("z", unit)
        theirs = block(unit, 1, 0)
        send(("r1", unit), theirs, theirs, at(dy=1))
        send(("l1", unit), theirs, theirs, at(dy=3))

    def ring(unit):
        arrived("r0", unit)
        left = block(unit, 0, 3)
        send(("f0", unit), left, left, at(dy=1))
        arrived("l1", unit)
        right = block(unit, 1, 1)
        send(("f1", unit), right, right, at(dy=3))

    def turn(unit):
        right_way = CROSS.index(unit) % 2 == 0
        arrived("r0", unit)
        left = block(unit, 0, 3)
        if right_way:
            send(("f0", unit), left, left, at(dy=1))
        send(("zl", unit), left, left, at(dzl=1))
        arrived("l0", unit)
        right = block(unit, 0, 1)
        if not right_way:
            send(("f0", unit), right, right, at(dy=3))
        send(("zr", unit), right, right, at(dzl=1))

    def cross(unit):
        arrived("f0", unit)
        far = block(unit, 0, 2)
        send(("zf", unit), far, far, at(dzl=1))

    stores = []

    def store(unit):
        for name in ("z", "zl", "zr", "zf") if unit in CROSS else ("l0", "r1", "f0", "f1"):
            arrived(name, unit)
        part = pl.ds(plane_at(*unit) * NAGE, NAGE)
        copy = pltpu.make_async_copy(comp.at[part], out_ref.at[part], out_sem.at[len(stores)])
        copy.start()
        stores.append(copy)

    def own(half):
        for k in range(half * 4, half * 4 + 4):
            pltpu.make_async_copy(w_ref.at[pl.ds(0, HALF)], wall.at[plane, core, k], a1_recv.at[k]).wait()

    for kind, what in schedule():
        if kind == "send":
            send_weights(*what)
        elif kind == "take":
            take_weights(*what)
        elif kind == "own":
            own(what)
        elif kind == "pass":
            pass_on(*what)
        elif kind == "library":
            library(what)
        elif kind == "compose":
            compose(what)
        elif kind == "pair":
            pair(what)
        elif kind == "ring":
            ring(what)
        elif kind == "turn":
            turn(what)
        elif kind == "cross":
            cross(what)
        else:
            store(what)

    for n, dy in enumerate(FAR_FIRST):
        for h in range(2):
            mine = jnp.logical_and(core == h, core * 4 + lax.rem(y + dy, NY) == age)

            @pl.when(jnp.logical_not(mine))
            def _():
                rows = w_ref.at[pl.ds(0, HALF)]
                pltpu.make_async_copy(rows, wall.at[plane, core, 0], a1_send.at[n * 2 + h]).wait()

    for copy in copies.values():
        copy.wait_send()
    for copy in stores:
        copy.wait()
    bring.wait()


def composites(weights, library_t, kernels_t):
    n_copies = 7 + 30 + 32 + 7 * 16
    return pl.pallas_call(
        gather_kernel,
        out_shape=[
            jax.ShapeDtypeStruct((NPLANE * NAGE, WIN, ROWS), jnp.bfloat16),
            jax.ShapeDtypeStruct(kernels_t.shape, kernels_t.dtype),
        ],
        in_specs=[pl.BlockSpec(memory_space=pltpu.HBM)] * 3,
        out_specs=[pl.BlockSpec(memory_space=pl.ANY)] * 2,
        scratch_shapes=[
            pltpu.VMEM((NPLANE, 2, NAGE, HALF, KB), jnp.bfloat16),
            pltpu.VMEM((NAGE, WIN, KB), jnp.bfloat16),
            pltpu.VMEM((NPLANE * NAGE, WIN, ROWS), jnp.bfloat16),
            pltpu.SemaphoreType.DMA((n_copies,)),
            pltpu.SemaphoreType.DMA((n_copies,)),
            pltpu.SemaphoreType.DMA((8,)),
            pltpu.SemaphoreType.DMA((8,)),
            pltpu.SemaphoreType.DMA,
            pltpu.SemaphoreType.DMA,
            pltpu.SemaphoreType.DMA((NPLANE,)),
        ],
        compiler_params=pltpu.CompilerParams(
            collective_id=0, has_side_effects=True, vmem_limit_bytes=24 * 1024 * 1024
        ),
        cost_estimate=pl.CostEstimate(
            flops=2 * 2048 * 2048 * WIN, bytes_accessed=6 * 1024 * 1024, transcendentals=0
        ),
        name="composites",
    )(weights, library_t, kernels_t)


BLOCKS = 32


def photometry_kernel(k_ref, c_ref, o_ref):
    n_z, n_f, n_w = k_ref.shape
    kern = k_ref[...].reshape(n_z * n_f, n_w)
    first = pl.program_id(0) * BLOCKS
    for b in range(0, BLOCKS, 2):
        cols = jnp.concatenate([c_ref[first + b], c_ref[first + b + 1]], axis=1)
        flux = jnp.dot(kern, cols, preferred_element_type=jnp.float32).astype(jnp.bfloat16)
        o_ref[:, :, b * ROWS:(b + 2) * ROWS] = flux.reshape(n_z, n_f, 2 * ROWS)


def photometry(kernels_t, composite):
    n_z, n_f, n_w = kernels_t.shape
    n_blocks = composite.shape[0]
    return pl.pallas_call(
        photometry_kernel,
        grid=(n_blocks // BLOCKS,),
        out_shape=jax.ShapeDtypeStruct((n_z, n_f, n_blocks * ROWS), jnp.bfloat16),
        in_specs=[
            pl.BlockSpec(memory_space=pltpu.VMEM),
            pl.BlockSpec(memory_space=pltpu.VMEM),
        ],
        out_specs=pl.BlockSpec((n_z, n_f, BLOCKS * ROWS), lambda i: (0, 0, i)),
        compiler_params=pltpu.CompilerParams(vmem_limit_bytes=24 * 1024 * 1024),
        name="photometry",
    )(kernels_t, composite)


def local(sfh_weights, library, kernels):
    inputs = (sfh_weights, library.T, kernels.transpose(0, 2, 1))
    composite, kernels_t = composites(*[pltpu.with_memory_space_constraint(a, pltpu.HBM) for a in inputs])
    fluxes = photometry(kernels_t, composite)
    return fluxes.transpose(0, 2, 1)


def solution(mesh):
    placed = (P("sfh", "age"), P("age", "sfh"), P(("age", "sfh"), None, None))
    return jax.shard_map(
        local, mesh=mesh, in_specs=placed, out_specs=P(("age", "sfh"), None, None), check_vma=False
    )
```

```python
import functools

import jax
import jax.numpy as jnp
from jax import lax
from jax.experimental import pallas as pl
from jax.experimental.pallas import tpu as pltpu
from jax.sharding import PartitionSpec as P

MESH = pl.DeviceIdType.MESH

NY, NX, NZH = 4, 4, 4
NAGE, NPLANE = 8, 16
ROWS = 128
HALF = 64
KB = 256
WIN = 160

SENT = {
    "x+": [((0, 0), 0), ((0, 0), 1), ((0, 3), 0), ((3, 0), 0), ((1, 0), 1), ((3, 0), 1),
           ((1, 0), 0), ((3, 3), 0), ((1, 3), 0), ((2, 0), 0), ((2, 0), 1), ((2, 3), 0)],
    "x-": [((0, 0), 1), ((0, 0), 0), ((0, 1), 1), ((1, 0), 1), ((3, 0), 0), ((1, 0), 0),
           ((3, 0), 1), ((1, 1), 1), ((3, 1), 1), ((2, 0), 1), ((2, 0), 0), ((2, 1), 1)],
    "z+": [((0, 0), 0), ((0, 0), 1), ((3, 0), 0)],
    "z-": [((0, 0), 1), ((0, 0), 0), ((1, 0), 1)],
}
STEP = {"x+": (0, 1), "x-": (0, 3), "z+": (1, 0), "z-": (3, 0)}
UNITS = [(0, 0), (0, 3), (0, 1), (0, 2), (3, 0), (1, 0), (3, 3), (1, 1),
         (1, 3), (3, 1), (2, 0), (3, 2), (1, 2), (2, 3), (2, 1), (2, 2)]
CROSS = ((0, 1), (3, 0), (1, 1), (3, 1), (3, 2), (2, 3))
AHEAD = 2
FAR_FIRST = (2, 1, 3, 0)
Z_SEND, Z_RECV = (-0.05, 1.0, 2.9), (2.85, 4.85, 8.8)
LIBRARY, TURN, FIRST, PACE = 0.05, 0.8, 2.2, 0.65
PAIR_LAG, RING_LAG, STORE_LAG = 2.0, 4.0, 10.0
SETTLE = 0.5


def schedule():
    events = []
    for n in range(12):
        events.append((n or -0.24, "send", ("x+", n)))
        events.append((n or -0.04, "send", ("x-", n)))
        events.append((n + AHEAD - 0.1, "take", ("x+", n)))
        events.append((n + AHEAD - 0.1, "take", ("x-", n)))
    for n in range(3):
        for way in ("z+", "z-"):
            early = 0.2 if (way, n) == ("z+", 0) else 0.0
            events.append((Z_SEND[n] - early, "send", (way, n)))
            events.append((Z_RECV[n], "take", (way, n)))
    events += [(-0.3, "own", 0), (-0.2, "own", 1)]
    events += [(0.01, "pass", ((0, 0), half)) for half in range(2)]
    events.append((LIBRARY, "library", "pass"))
    events.append((TURN, "library", "turn"))
    events.append((FIRST - 0.01, "library", "wait"))
    ready = {}
    for moment, kind, what in events:
        if kind == "take":
            (dz, dx), _ = SENT[what[0]][what[1]]
            unit = ((dz - STEP[what[0]][0]) % 4, (dx - STEP[what[0]][1]) % 4)
            ready[unit] = max(ready.get(unit, 0.0), moment + SETTLE)
    now = FIRST - PACE
    for unit in UNITS:
        now = max(now + PACE, ready.get(unit, 0.0))
        events.append((now, "compose", unit))
        events.append((now + PAIR_LAG, "turn" if unit in CROSS else "pair", unit))
        events.append((now + RING_LAG, "cross" if unit in CROSS else "ring", unit))
        events.append((now + STORE_LAG, "store", unit))
    order = sorted(range(len(events)), key=lambda e: events[e][0])
    return [events[e][1:] for e in order]


def gather_kernel(
    w_ref, l_ref, k_ref, out_ref, k_out, wall, lib, comp, ssem, rsem, a1_send, a1_recv, lib_sem, k_sem, out_sem
):
    age = lax.axis_index("age")
    sfh = lax.axis_index("sfh")
    zl, y = lax.div(age, NY), lax.rem(age, NY)
    core = lax.rem(sfh, 2)
    plane = lax.div(sfh, 2)
    zh, x = lax.div(plane, NX), lax.rem(plane, NX)

    def at(dzl=0, dy=0, dzh=0, dx=0, dc=0):
        a = lax.rem(zl + dzl, 2) * NY + lax.rem(y + dy, NY)
        s = (lax.rem(zh + dzh, NZH) * NX + lax.rem(x + dx, NX)) * 2 + lax.rem(core + dc, 2)
        return (a, s)

    def plane_at(dz, dx):
        return lax.rem(zh + dz, NZH) * NX + lax.rem(x + dx, NX)

    def position(other, dy):
        return lax.rem(zl + other, 2) * NY + lax.rem(y + dy, NY)

    barrier = pltpu.get_barrier_semaphore()
    partners = [at(dzl, dy, 0, 0, dc) for dzl in range(2) for dy in range(NY) for dc in range(2) if (dzl, dy, dc) != (0, 0, 0)]
    partners += [at(dx=1), at(dx=3), at(dzh=1), at(dzh=3)]
    for partner in partners:
        pl.semaphore_signal(barrier, inc=1, device_id=partner, device_id_type=MESH)
    pl.semaphore_wait(barrier, len(partners))

    copies = {}

    def send(name, src, dst, to):
        index = len(copies)
        copy = pltpu.make_async_remote_copy(
            src_ref=src, dst_ref=dst, send_sem=ssem.at[index], recv_sem=rsem.at[index],
            device_id=to, device_id_type=MESH,
        )
        copy.start()
        copies[name] = copy

    def arrived(*name):
        copies[name].wait_recv()

    for n, dy in enumerate(FAR_FIRST):
        q = lax.rem(y + dy, NY)
        r = core * 4 + q
        for h in range(2):
            src = w_ref.at[pl.ds(pl.multiple_of(q * ROWS + h * HALF, HALF), HALF)]
            dst = wall.at[plane, h, age]
            mine = jnp.logical_and(core == h, r == age)

            @pl.when(mine)
            def _():
                pltpu.make_async_copy(src, dst, a1_recv.at[age]).start()

            @pl.when(jnp.logical_not(mine))
            def _():
                pltpu.make_async_remote_copy(
                    src_ref=src, dst_ref=dst, send_sem=a1_send.at[n * 2 + h], recv_sem=a1_recv.at[age],
                    device_id=(r, plane * 2 + h), device_id_type=MESH,
                ).start()

    own_lib = pltpu.make_async_copy(l_ref, lib.at[age], lib_sem)
    own_lib.start()
    bring = pltpu.make_async_copy(k_ref, k_out, k_sem)
    bring.start()
    send(("lib", "z"), l_ref, lib.at[age], at(dzl=1))
    send(("lib", "r0"), l_ref, lib.at[age], at(dy=1))
    send(("lib", "l0"), l_ref, lib.at[age], at(dy=3))

    def library(what):
        if what == "pass":
            arrived("lib", "z")
            theirs = lib.at[position(1, 0)]
            send(("lib", "r1"), theirs, theirs, at(dy=1))
            send(("lib", "l1"), theirs, theirs, at(dy=3))
            arrived("lib", "r0")
            left = lib.at[position(0, 3)]
            send(("lib", "f0"), left, left, at(dy=1))
        elif what == "turn":
            arrived("lib", "l1")
            right = lib.at[position(1, 1)]
            send(("lib", "f1"), right, right, at(dy=3))
        else:
            own_lib.wait()
            for name in ("l0", "r1", "f0", "f1"):
                arrived("lib", name)

    def pass_on(unit, half):
        part = wall.at[plane_at(*unit), core, pl.ds(half * 4, 4)]
        send(("core", unit, half), part, part, at(dc=1))

    def send_weights(way, n):
        unit, half = SENT[way][n]
        part = wall.at[plane_at(*unit), core, pl.ds(half * 4, 4)]
        dz, dx = STEP[way]
        send((way, n), part, part, at(dzh=dz, dx=dx))

    def take_weights(way, n):
        (dz, dx), half = SENT[way][n]
        arrived(way, n)
        pass_on(((dz - STEP[way][0]) % 4, (dx - STEP[way][1]) % 4), half)

    def block(unit, other, dy):
        return comp.at[plane_at(*unit) * NAGE + position(other, dy)]

    def compose(unit):
        arrived("core", unit, 0)
        arrived("core", unit, 1)
        p = plane_at(*unit)
        total = jnp.zeros((WIN, ROWS), jnp.float32)
        for k in range(NAGE):
            rows = wall[p, :, k].reshape(ROWS, KB)
            total += lax.dot_general(lib[k], rows, (((1,), (1,)), ((), ())), preferred_element_type=jnp.float32)
        comp[p * NAGE + age] = total.astype(jnp.bfloat16)
        mine = block(unit, 0, 0)
        send(("z", unit), mine, mine, at(dzl=1))
        send(("r0", unit), mine, mine, at(dy=1))
        send(("l0", unit), mine, mine, at(dy=3))

    def pair(unit):
        arrived("z", unit)
        theirs = block(unit, 1, 0)
        send(("r1", unit), theirs, theirs, at(dy=1))
        send(("l1", unit), theirs, theirs, at(dy=3))

    def ring(unit):
        arrived("r0", unit)
        left = block(unit, 0, 3)
        send(("f0", unit), left, left, at(dy=1))
        arrived("l1", unit)
        right = block(unit, 1, 1)
        send(("f1", unit), right, right, at(dy=3))

    def turn(unit):
        right_way = CROSS.index(unit) % 2 == 0
        arrived("r0", unit)
        left = block(unit, 0, 3)
        if right_way:
            send(("f0", unit), left, left, at(dy=1))
        send(("zl", unit), left, left, at(dzl=1))
        arrived("l0", unit)
        right = block(unit, 0, 1)
        if not right_way:
            send(("f0", unit), right, right, at(dy=3))
        send(("zr", unit), right, right, at(dzl=1))

    def cross(unit):
        arrived("f0", unit)
        far = block(unit, 0, 2)
        send(("zf", unit), far, far, at(dzl=1))

    stores = []

    def store(unit):
        for name in ("z", "zl", "zr", "zf") if unit in CROSS else ("l0", "r1", "f0", "f1"):
            arrived(name, unit)
        part = pl.ds(plane_at(*unit) * NAGE, NAGE)
        copy = pltpu.make_async_copy(comp.at[part], out_ref.at[part], out_sem.at[len(stores)])
        copy.start()
        stores.append(copy)

    def own(half):
        for k in range(half * 4, half * 4 + 4):
            pltpu.make_async_copy(w_ref.at[pl.ds(0, HALF)], wall.at[plane, core, k], a1_recv.at[k]).wait()

    for kind, what in schedule():
        if kind == "send":
            send_weights(*what)
        elif kind == "take":
            take_weights(*what)
        elif kind == "own":
            own(what)
        elif kind == "pass":
            pass_on(*what)
        elif kind == "library":
            library(what)
        elif kind == "compose":
            compose(what)
        elif kind == "pair":
            pair(what)
        elif kind == "ring":
            ring(what)
        elif kind == "turn":
            turn(what)
        elif kind == "cross":
            cross(what)
        else:
            store(what)

    for n, dy in enumerate(FAR_FIRST):
        for h in range(2):
            mine = jnp.logical_and(core == h, core * 4 + lax.rem(y + dy, NY) == age)

            @pl.when(jnp.logical_not(mine))
            def _():
                rows = w_ref.at[pl.ds(0, HALF)]
                pltpu.make_async_copy(rows, wall.at[plane, core, 0], a1_send.at[n * 2 + h]).wait()

    for copy in copies.values():
        copy.wait_send()
    for copy in stores:
        copy.wait()
    bring.wait()


def composites(weights, library_t, kernels_t):
    n_copies = 7 + 30 + 32 + 7 * 16
    return pl.pallas_call(
        gather_kernel,
        out_shape=[
            jax.ShapeDtypeStruct((NPLANE * NAGE, WIN, ROWS), jnp.bfloat16),
            jax.ShapeDtypeStruct(kernels_t.shape, kernels_t.dtype),
        ],
        in_specs=[pl.BlockSpec(memory_space=pltpu.HBM)] * 3,
        out_specs=[pl.BlockSpec(memory_space=pl.ANY)] * 2,
        scratch_shapes=[
            pltpu.VMEM((NPLANE, 2, NAGE, HALF, KB), jnp.bfloat16),
            pltpu.VMEM((NAGE, WIN, KB), jnp.bfloat16),
            pltpu.VMEM((NPLANE * NAGE, WIN, ROWS), jnp.bfloat16),
            pltpu.SemaphoreType.DMA((n_copies,)),
            pltpu.SemaphoreType.DMA((n_copies,)),
            pltpu.SemaphoreType.DMA((8,)),
            pltpu.SemaphoreType.DMA((8,)),
            pltpu.SemaphoreType.DMA,
            pltpu.SemaphoreType.DMA,
            pltpu.SemaphoreType.DMA((NPLANE,)),
        ],
        compiler_params=pltpu.CompilerParams(
            collective_id=0, has_side_effects=True, vmem_limit_bytes=24 * 1024 * 1024
        ),
        cost_estimate=pl.CostEstimate(
            flops=2 * 2048 * 2048 * WIN, bytes_accessed=6 * 1024 * 1024, transcendentals=0
        ),
        name="composites",
    )(weights, library_t, kernels_t)


BLOCKS = 64


def photometry_kernel(k_ref, c_ref, o_ref):
    n_z, n_f, n_w = k_ref.shape
    kern = k_ref[...].reshape(n_z * n_f, n_w)
    first = pl.program_id(0) * BLOCKS
    for b in range(0, BLOCKS, 2):
        cols = jnp.concatenate([c_ref[first + b], c_ref[first + b + 1]], axis=1)
        flux = jnp.dot(kern, cols, preferred_element_type=jnp.float32).astype(jnp.bfloat16)
        o_ref[:, :, b * ROWS:(b + 2) * ROWS] = flux.reshape(n_z, n_f, 2 * ROWS)


def photometry(kernels_t, composite):
    n_z, n_f, n_w = kernels_t.shape
    n_blocks = composite.shape[0]
    return pl.pallas_call(
        photometry_kernel,
        grid=(n_blocks // BLOCKS,),
        out_shape=jax.ShapeDtypeStruct((n_z, n_f, n_blocks * ROWS), jnp.bfloat16),
        in_specs=[
            pl.BlockSpec(memory_space=pltpu.VMEM),
            pl.BlockSpec(memory_space=pltpu.VMEM),
        ],
        out_specs=pl.BlockSpec((n_z, n_f, BLOCKS * ROWS), lambda i: (0, 0, i)),
        compiler_params=pltpu.CompilerParams(vmem_limit_bytes=24 * 1024 * 1024),
        name="photometry",
    )(kernels_t, composite)


def local(sfh_weights, library, kernels):
    inputs = (sfh_weights, library.T, kernels.transpose(0, 2, 1))
    composite, kernels_t = composites(*[pltpu.with_memory_space_constraint(a, pltpu.HBM) for a in inputs])
    fluxes = photometry(kernels_t, composite)
    return fluxes.transpose(0, 2, 1)


def solution(mesh):
    placed = (P("sfh", "age"), P("age", "sfh"), P(("age", "sfh"), None, None))
    return jax.shard_map(
        local, mesh=mesh, in_specs=placed, out_specs=P(("age", "sfh"), None, None), check_vma=False
    )
```

```python
import functools

import jax
import jax.numpy as jnp
from jax import lax
from jax.experimental import pallas as pl
from jax.experimental.pallas import tpu as pltpu
from jax.sharding import PartitionSpec as P

MESH = pl.DeviceIdType.MESH

NY, NX, NZH = 4, 4, 4
NAGE, NPLANE = 8, 16
ROWS = 128
HALF = 64
KB = 256
WIN = 160

SENT = {
    "x+": [((0, 0), 0), ((0, 0), 1), ((0, 3), 0), ((3, 0), 0), ((1, 0), 1), ((3, 0), 1),
           ((1, 0), 0), ((3, 3), 0), ((1, 3), 0), ((2, 0), 0), ((2, 0), 1), ((2, 3), 0)],
    "x-": [((0, 0), 1), ((0, 0), 0), ((0, 1), 1), ((1, 0), 1), ((3, 0), 0), ((1, 0), 0),
           ((3, 0), 1), ((1, 1), 1), ((3, 1), 1), ((2, 0), 1), ((2, 0), 0), ((2, 1), 1)],
    "z+": [((0, 0), 0), ((0, 0), 1), ((3, 0), 0)],
    "z-": [((0, 0), 1), ((0, 0), 0), ((1, 0), 1)],
}
STEP = {"x+": (0, 1), "x-": (0, 3), "z+": (1, 0), "z-": (3, 0)}
UNITS = [(0, 0), (0, 3), (0, 1), (0, 2), (3, 0), (1, 0), (3, 3), (1, 1),
         (1, 3), (3, 1), (2, 0), (3, 2), (1, 2), (2, 3), (2, 1), (2, 2)]
CROSS = ((0, 1), (3, 0), (1, 1), (3, 1), (3, 2), (2, 3))
AHEAD = 2
FAR_FIRST = (2, 1, 3, 0)
Z_SEND, Z_RECV = (-0.05, 1.0, 2.9), (2.85, 4.85, 8.8)
LIBRARY, TURN, FIRST, PACE = 0.05, 0.8, 2.2, 0.65
PAIR_LAG, RING_LAG, STORE_LAG = 2.0, 4.0, 8.0
SETTLE = 0.5


def schedule():
    events = []
    for n in range(12):
        events.append((n or -0.24, "send", ("x+", n)))
        events.append((n or -0.04, "send", ("x-", n)))
        events.append((n + AHEAD - 0.1, "take", ("x+", n)))
        events.append((n + AHEAD - 0.1, "take", ("x-", n)))
    for n in range(3):
        for way in ("z+", "z-"):
            early = 0.2 if (way, n) == ("z+", 0) else 0.0
            events.append((Z_SEND[n] - early, "send", (way, n)))
            events.append((Z_RECV[n], "take", (way, n)))
    events += [(-0.3, "own", 0), (-0.2, "own", 1)]
    events += [(0.01, "pass", ((0, 0), half)) for half in range(2)]
    events.append((LIBRARY, "library", "pass"))
    events.append((TURN, "library", "turn"))
    events.append((FIRST - 0.01, "library", "wait"))
    ready = {}
    for moment, kind, what in events:
        if kind == "take":
            (dz, dx), _ = SENT[what[0]][what[1]]
            unit = ((dz - STEP[what[0]][0]) % 4, (dx - STEP[what[0]][1]) % 4)
            ready[unit] = max(ready.get(unit, 0.0), moment + SETTLE)
    now = FIRST - PACE
    for unit in UNITS:
        now = max(now + PACE, ready.get(unit, 0.0))
        events.append((now, "compose", unit))
        events.append((now + PAIR_LAG, "turn" if unit in CROSS else "pair", unit))
        events.append((now + RING_LAG, "cross" if unit in CROSS else "ring", unit))
        events.append((now + STORE_LAG, "store", unit))
    order = sorted(range(len(events)), key=lambda e: events[e][0])
    return [events[e][1:] for e in order]


def gather_kernel(
    w_ref, l_ref, k_ref, out_ref, k_out, wall, lib, comp, ssem, rsem, a1_send, a1_recv, lib_sem, k_sem, out_sem
):
    age = lax.axis_index("age")
    sfh = lax.axis_index("sfh")
    zl, y = lax.div(age, NY), lax.rem(age, NY)
    core = lax.rem(sfh, 2)
    plane = lax.div(sfh, 2)
    zh, x = lax.div(plane, NX), lax.rem(plane, NX)

    def at(dzl=0, dy=0, dzh=0, dx=0, dc=0):
        a = lax.rem(zl + dzl, 2) * NY + lax.rem(y + dy, NY)
        s = (lax.rem(zh + dzh, NZH) * NX + lax.rem(x + dx, NX)) * 2 + lax.rem(core + dc, 2)
        return (a, s)

    def plane_at(dz, dx):
        return lax.rem(zh + dz, NZH) * NX + lax.rem(x + dx, NX)

    def position(other, dy):
        return lax.rem(zl + other, 2) * NY + lax.rem(y + dy, NY)

    barrier = pltpu.get_barrier_semaphore()
    partners = [at(dzl, dy, 0, 0, dc) for dzl in range(2) for dy in range(NY) for dc in range(2) if (dzl, dy, dc) != (0, 0, 0)]
    partners += [at(dx=1), at(dx=3), at(dzh=1), at(dzh=3)]
    for partner in partners:
        pl.semaphore_signal(barrier, inc=1, device_id=partner, device_id_type=MESH)
    pl.semaphore_wait(barrier, len(partners))

    copies = {}

    def send(name, src, dst, to):
        index = len(copies)
        copy = pltpu.make_async_remote_copy(
            src_ref=src, dst_ref=dst, send_sem=ssem.at[index], recv_sem=rsem.at[index],
            device_id=to, device_id_type=MESH,
        )
        copy.start()
        copies[name] = copy

    def arrived(*name):
        copies[name].wait_recv()

    for n, dy in enumerate(FAR_FIRST):
        q = lax.rem(y + dy, NY)
        r = core * 4 + q
        for h in range(2):
            src = w_ref.at[pl.ds(pl.multiple_of(q * ROWS + h * HALF, HALF), HALF)]
            dst = wall.at[plane, h, age]
            mine = jnp.logical_and(core == h, r == age)

            @pl.when(mine)
            def _():
                pltpu.make_async_copy(src, dst, a1_recv.at[age]).start()

            @pl.when(jnp.logical_not(mine))
            def _():
                pltpu.make_async_remote_copy(
                    src_ref=src, dst_ref=dst, send_sem=a1_send.at[n * 2 + h], recv_sem=a1_recv.at[age],
                    device_id=(r, plane * 2 + h), device_id_type=MESH,
                ).start()

    own_lib = pltpu.make_async_copy(l_ref, lib.at[age], lib_sem)
    own_lib.start()
    bring = pltpu.make_async_copy(k_ref, k_out, k_sem)
    bring.start()
    send(("lib", "z"), l_ref, lib.at[age], at(dzl=1))
    send(("lib", "r0"), l_ref, lib.at[age], at(dy=1))
    send(("lib", "l0"), l_ref, lib.at[age], at(dy=3))

    def library(what):
        if what == "pass":
            arrived("lib", "z")
            theirs = lib.at[position(1, 0)]
            send(("lib", "r1"), theirs, theirs, at(dy=1))
            send(("lib", "l1"), theirs, theirs, at(dy=3))
            arrived("lib", "r0")
            left = lib.at[position(0, 3)]
            send(("lib", "f0"), left, left, at(dy=1))
        elif what == "turn":
            arrived("lib", "l1")
            right = lib.at[position(1, 1)]
            send(("lib", "f1"), right, right, at(dy=3))
        else:
            own_lib.wait()
            for name in ("l0", "r1", "f0", "f1"):
                arrived("lib", name)

    def pass_on(unit, half):
        part = wall.at[plane_at(*unit), core, pl.ds(half * 4, 4)]
        send(("core", unit, half), part, part, at(dc=1))

    def send_weights(way, n):
        unit, half = SENT[way][n]
        part = wall.at[plane_at(*unit), core, pl.ds(half * 4, 4)]
        dz, dx = STEP[way]
        send((way, n), part, part, at(dzh=dz, dx=dx))

    def take_weights(way, n):
        (dz, dx), half = SENT[way][n]
        arrived(way, n)
        pass_on(((dz - STEP[way][0]) % 4, (dx - STEP[way][1]) % 4), half)

    def block(unit, other, dy):
        return comp.at[plane_at(*unit) * NAGE + position(other, dy)]

    def compose(unit):
        arrived("core", unit, 0)
        arrived("core", unit, 1)
        p = plane_at(*unit)
        total = jnp.zeros((WIN, ROWS), jnp.float32)
        for k in range(NAGE):
            rows = wall[p, :, k].reshape(ROWS, KB)
            total += lax.dot_general(lib[k], rows, (((1,), (1,)), ((), ())), preferred_element_type=jnp.float32)
        comp[p * NAGE + age] = total.astype(jnp.bfloat16)
        mine = block(unit, 0, 0)
        send(("z", unit), mine, mine, at(dzl=1))
        send(("r0", unit), mine, mine, at(dy=1))
        send(("l0", unit), mine, mine, at(dy=3))

    def pair(unit):
        arrived("z", unit)
        theirs = block(unit, 1, 0)
        send(("r1", unit), theirs, theirs, at(dy=1))
        send(("l1", unit), theirs, theirs, at(dy=3))

    def ring(unit):
        arrived("r0", unit)
        left = block(unit, 0, 3)
        send(("f0", unit), left, left, at(dy=1))
        arrived("l1", unit)
        right = block(unit, 1, 1)
        send(("f1", unit), right, right, at(dy=3))

    def turn(unit):
        right_way = CROSS.index(unit) % 2 == 0
        arrived("r0", unit)
        left = block(unit, 0, 3)
        if right_way:
            send(("f0", unit), left, left, at(dy=1))
        send(("zl", unit), left, left, at(dzl=1))
        arrived("l0", unit)
        right = block(unit, 0, 1)
        if not right_way:
            send(("f0", unit), right, right, at(dy=3))
        send(("zr", unit), right, right, at(dzl=1))

    def cross(unit):
        arrived("f0", unit)
        far = block(unit, 0, 2)
        send(("zf", unit), far, far, at(dzl=1))

    stores = []

    def store(unit):
        for name in ("z", "zl", "zr", "zf") if unit in CROSS else ("l0", "r1", "f0", "f1"):
            arrived(name, unit)
        part = pl.ds(plane_at(*unit) * NAGE, NAGE)
        copy = pltpu.make_async_copy(comp.at[part], out_ref.at[part], out_sem.at[len(stores)])
        copy.start()
        stores.append(copy)

    def own(half):
        for k in range(half * 4, half * 4 + 4):
            pltpu.make_async_copy(w_ref.at[pl.ds(0, HALF)], wall.at[plane, core, k], a1_recv.at[k]).wait()

    for kind, what in schedule():
        if kind == "send":
            send_weights(*what)
        elif kind == "take":
            take_weights(*what)
        elif kind == "own":
            own(what)
        elif kind == "pass":
            pass_on(*what)
        elif kind == "library":
            library(what)
        elif kind == "compose":
            compose(what)
        elif kind == "pair":
            pair(what)
        elif kind == "ring":
            ring(what)
        elif kind == "turn":
            turn(what)
        elif kind == "cross":
            cross(what)
        else:
            store(what)

    for n, dy in enumerate(FAR_FIRST):
        for h in range(2):
            mine = jnp.logical_and(core == h, core * 4 + lax.rem(y + dy, NY) == age)

            @pl.when(jnp.logical_not(mine))
            def _():
                rows = w_ref.at[pl.ds(0, HALF)]
                pltpu.make_async_copy(rows, wall.at[plane, core, 0], a1_send.at[n * 2 + h]).wait()

    for copy in copies.values():
        copy.wait_send()
    for copy in stores:
        copy.wait()
    bring.wait()


def composites(weights, library_t, kernels_t):
    n_copies = 7 + 30 + 32 + 7 * 16
    return pl.pallas_call(
        gather_kernel,
        out_shape=[
            jax.ShapeDtypeStruct((NPLANE * NAGE, WIN, ROWS), jnp.bfloat16),
            jax.ShapeDtypeStruct(kernels_t.shape, kernels_t.dtype),
        ],
        in_specs=[pl.BlockSpec(memory_space=pltpu.HBM)] * 3,
        out_specs=[pl.BlockSpec(memory_space=pl.ANY)] * 2,
        scratch_shapes=[
            pltpu.VMEM((NPLANE, 2, NAGE, HALF, KB), jnp.bfloat16),
            pltpu.VMEM((NAGE, WIN, KB), jnp.bfloat16),
            pltpu.VMEM((NPLANE * NAGE, WIN, ROWS), jnp.bfloat16),
            pltpu.SemaphoreType.DMA((n_copies,)),
            pltpu.SemaphoreType.DMA((n_copies,)),
            pltpu.SemaphoreType.DMA((8,)),
            pltpu.SemaphoreType.DMA((8,)),
            pltpu.SemaphoreType.DMA,
            pltpu.SemaphoreType.DMA,
            pltpu.SemaphoreType.DMA((NPLANE,)),
        ],
        compiler_params=pltpu.CompilerParams(
            collective_id=0, has_side_effects=True, vmem_limit_bytes=24 * 1024 * 1024
        ),
        cost_estimate=pl.CostEstimate(
            flops=2 * 2048 * 2048 * WIN, bytes_accessed=6 * 1024 * 1024, transcendentals=0
        ),
        name="composites",
    )(weights, library_t, kernels_t)


BLOCKS = 32


def photometry_kernel(k_ref, c_ref, o_ref):
    n_z, n_f, n_w = k_ref.shape
    kern = k_ref[...].reshape(n_z * n_f, n_w)
    first = pl.program_id(0) * BLOCKS
    for b in range(0, BLOCKS, 2):
        cols = jnp.concatenate([c_ref[first + b], c_ref[first + b + 1]], axis=1)
        flux = jnp.dot(kern, cols, preferred_element_type=jnp.float32).astype(jnp.bfloat16)
        o_ref[:, :, b * ROWS:(b + 2) * ROWS] = flux.reshape(n_z, n_f, 2 * ROWS)


def photometry(kernels_t, composite):
    n_z, n_f, n_w = kernels_t.shape
    n_blocks = composite.shape[0]
    return pl.pallas_call(
        photometry_kernel,
        grid=(n_blocks // BLOCKS,),
        out_shape=jax.ShapeDtypeStruct((n_z, n_f, n_blocks * ROWS), jnp.bfloat16),
        in_specs=[
            pl.BlockSpec(memory_space=pltpu.VMEM),
            pl.BlockSpec(memory_space=pltpu.VMEM),
        ],
        out_specs=pl.BlockSpec((n_z, n_f, BLOCKS * ROWS), lambda i: (0, 0, i)),
        compiler_params=pltpu.CompilerParams(vmem_limit_bytes=24 * 1024 * 1024),
        name="photometry",
    )(kernels_t, composite)


def local(sfh_weights, library, kernels):
    inputs = (sfh_weights, library.T, kernels.transpose(0, 2, 1))
    composite, kernels_t = composites(*[pltpu.with_memory_space_constraint(a, pltpu.HBM) for a in inputs])
    fluxes = photometry(kernels_t, composite)
    return fluxes.transpose(0, 2, 1)


def solution(mesh):
    placed = (P("sfh", "age"), P("age", "sfh"), P(("age", "sfh"), None, None))
    return jax.shard_map(
        local, mesh=mesh, in_specs=placed, out_specs=P(("age", "sfh"), None, None), check_vma=False
    )
```
